256 devices in a mesh: cent: 32 (over z, x_lo, core), row: 8 (over y, x_hi).
Axes of the slice: x: 4 (x_hi: 2, x_lo: 2; x = x_hi * 2 + x_lo), y: 4, z: 8, core: 2. Of those that a mesh axis runs over, the one named last changes fastest.
Arguments:
- points: bfloat16 [2048, 768], P('row', 'cent'), may hold values from -12.2 to 12.2
- centroids: bfloat16 [262144, 768], P(('cent', 'row')), may hold values from -4.5 to 4.5
Outputs:
- updated: bfloat16 [262144, 768], P(('cent', 'row'))
- log_partition: float32 [2048], P('row')
The draws below stay inside these ranges and needn't reach their ends.
All inputs are finite; a program needn't handle non-finite values.
Results may differ from the reference program's by a relative error of at most 0.001.
Values may be sent and summed in bfloat16 or wider, within the bound.
No kernel may reach another device: no remote copies, remote signals or barrier semaphores. Data moves between devices by JAX's collectives and lax.ppermute only.
A program may use at most 128 MiB of HBM per device.

```python
import math
import jax
import jax.numpy as jnp
from jax import lax

D = 768
KF = 262144
ROWS = 2048


def base_centroids(key):
    inner = jax.random.fold_in(key, 11)
    return jnp.clip(jax.random.normal(inner, (KF, D), jnp.float32), -4.5, 4.5)


def draw_centroids(key, part):
    values = base_centroids(key)
    return values.astype(jnp.bfloat16)


def draw_points(key, part):
    key = jax.random.fold_in(key, 5)
    first_key = jax.random.fold_in(key, 0)
    values = jnp.clip(jax.random.normal(first_key, (ROWS, D), jnp.float32), -4.5, 4.5)
    return values.astype(jnp.bfloat16)


def setup_inputs(seed: int = 0) -> dict:
    seeds = jax.random.split(jax.random.key(seed), 3)
    points = draw_points(jax.random.fold_in(seeds[2], 71), 0)
    centroids = draw_centroids(jax.random.fold_in(seeds[2], 71), 0)
    return {"points": points, "centroids": centroids}


def reference(points, centroids):
    sharpness = 4.0 / math.sqrt(D)
    block_size = min(4096, KF)
    block_count = KF // block_size
    cent_blocks = centroids.reshape(block_count, block_size, D)

    def statistics(carry, cent_block):
        highest, total = carry
        scores = sharpness * jnp.dot(points, cent_block.T, preferred_element_type=jnp.float32)
        fresh = jnp.maximum(highest, lax.optimization_barrier(jnp.max(scores, axis=1)))
        total = total * jnp.exp(highest - fresh) + lax.optimization_barrier(jnp.sum(jnp.exp(scores - fresh[:, None]), axis=1))
        return ((fresh, total), None)
    start = (jnp.full((ROWS,), -1e+30, jnp.float32), jnp.zeros((ROWS,), jnp.float32))
    (highest, total), _ = lax.scan(statistics, start, cent_blocks)
    log_partition = highest + jnp.log(total)

    def update_block(cent_block):
        scores = sharpness * jnp.dot(points, cent_block.T, preferred_element_type=jnp.float32)
        weights = jnp.exp(scores - log_partition[:, None]).astype(jnp.bfloat16)
        weight_mass = lax.optimization_barrier(jnp.sum(weights.astype(jnp.float32), axis=0))
        pulled = jnp.dot(weights.T, points, preferred_element_type=jnp.float32)
        return ((cent_block.astype(jnp.float32) + pulled) / (1.0 + weight_mass)[:, None]).astype(jnp.bfloat16)
    updated = lax.map(update_block, cent_blocks).reshape(KF, D)
    return (updated, log_partition)
```

```python
import itertools
import math

import jax
import jax.numpy as jnp
from jax import lax
from jax.experimental import pallas as pl
from jax.experimental.pallas import tpu as pltpu
from jax.sharding import Mesh
from jax.sharding import PartitionSpec as P

D = 768
AXES = ("z", "xl", "core", "y", "xh")
SIZES = {"z": 8, "xl": 2, "core": 2, "y": 4, "xh": 2}
LOG2E = math.log2(math.e)
LN2 = math.log(2.0)
SHARP2 = 4.0 / math.sqrt(D) * LOG2E
HALF = 128
ROWS = 256
GROUPS = 8


def permutation(move):
    places = list(itertools.product(*[range(SIZES[a]) for a in AXES]))
    number = {place: i for i, place in enumerate(places)}
    pairs = []
    for place in places:
        at = dict(zip(AXES, place))
        at["x"] = at["xh"] * 2 + at["xl"]
        src = move(at)
        src["xh"], src["xl"] = src["x"] // 2, src["x"] % 2
        pairs.append((number[tuple(src[a] for a in AXES)], number[place]))
    return pairs


def shifted(axis_of_core, step):
    def move(at):
        src = dict(at)
        axis = axis_of_core[at["core"]]
        src[axis] = (at[axis] + step) % 4
        return src

    return permutation(move)


def receive(value, pairs):
    return lax.ppermute(value, AXES, pairs)


FIRST = ("y", "x")
SECOND = ("x", "y")
SWAP = permutation(lambda at: {**at, "core": 1 - at["core"]})


def score_kernel(place, cents, *refs):
    pieces = refs[:10]
    points_t, scores, peak, total, sems = refs[10:]
    core = place[0]
    my_x = place[1]
    my_y = place[2]
    copies = []
    count = 0
    for other in range(2):
        side = core if other == 0 else 1 - core
        for index, (second, firsts) in enumerate(
            [(0, range(4)), (1, range(4)), (3, range(4)), (2, range(0, 2)), (2, range(2, 4))]
        ):
            src = pieces[other * 5 + index]
            for at, first in enumerate(firsts):
                dx = jnp.where(side == 0, second, first)
                dy = jnp.where(side == 0, first, second)
                x = lax.rem(my_x + dx, 4)
                y = lax.rem(my_y + dy, 4)
                group = y * 2 + lax.div(x, 2)
                copy = pltpu.make_async_copy(
                    src.at[at],
                    points_t.at[group, :, lax.rem(x, 2), :, pl.ds(pl.multiple_of(side * HALF, HALF), HALF)],
                    sems.at[count],
                )
                copy.start()
                copies.append(copy)
                count += 1
    for copy in copies:
        copy.wait()
    for group in range(GROUPS):
        block = points_t[group].reshape(D, ROWS)
        value = jnp.dot(cents[...], block, preferred_element_type=jnp.float32) * SHARP2
        top = jnp.max(value, axis=0, keepdims=True)
        scores[group] = value
        peak[pl.ds(group, 1), :] = top
        total[pl.ds(group, 1), :] = jnp.sum(jnp.exp2(value - top), axis=0, keepdims=True)


def pull_kernel(log_part, cents, points_t, scores, out):
    acc = None
    mass = None
    for group in range(GROUPS):
        block = points_t[group].reshape(D, ROWS)
        weights = jnp.exp2(scores[group] - log_part[pl.ds(group, 1), :]).astype(jnp.bfloat16)
        part = lax.dot_general(
            weights, block, (((1,), (1,)), ((), ())), preferred_element_type=jnp.float32
        )
        share = jnp.sum(weights.astype(jnp.float32), axis=1, keepdims=True)
        acc = part if acc is None else acc + part
        mass = share if mass is None else mass + share
    out[...] = ((cents[...].astype(jnp.float32) + acc) / (1.0 + mass)).astype(jnp.bfloat16)


def spread(value, axes, count):
    copies = jnp.broadcast_to(value[None], (count,) + value.shape)
    return lax.all_to_all(copies, axes, 0, 0, tiled=True)


def merge(pairs):
    peaks, totals = pairs[:, 0], pairs[:, 1]
    top = jnp.max(peaks, axis=0)
    return top, jnp.sum(totals * jnp.exp2(peaks - top[None]), axis=0)


def per_device(points, centroids):
    kept = centroids.shape[0]
    core = lax.axis_index("core")
    my_y = lax.axis_index("y")
    my_x = lax.axis_index("xh") * 2 + lax.axis_index("xl")

    feats = points.T
    halves = jnp.stack([feats[:, :HALF], feats[:, HALF:]])
    sent = jnp.broadcast_to(halves[None], (8,) + halves.shape).reshape((16,) + halves.shape[1:])
    got = lax.all_to_all(sent, ("z", "core"), 0, 0, tiled=True)
    own = got.reshape(8, 48, HALF)

    firsts = [own] + [receive(own, shifted(FIRST, k)) for k in (1, 2, 3)]
    line = jnp.stack(firsts)
    q0 = line
    q1 = receive(line, shifted(SECOND, 1))
    q3 = receive(line, shifted(SECOND, 3))
    q2a = receive(q1[:2], shifted(SECOND, 1))
    q2b = receive(q3[2:], shifted(SECOND, 3))
    mine = [q0, q1, q3, q2a, q2b]
    sibling = [receive(v, SWAP) for v in mine]

    place = jnp.stack([core, my_x, my_y]).astype(jnp.int32)
    any_space = pl.BlockSpec(memory_space=pl.ANY)
    vmem = pl.BlockSpec(memory_space=pltpu.VMEM)
    points_t, scores, peak, total = pl.pallas_call(
        score_kernel,
        out_shape=(
            jax.ShapeDtypeStruct((GROUPS, 8, 2, 48, ROWS), jnp.bfloat16),
            jax.ShapeDtypeStruct((GROUPS, kept, ROWS), jnp.float32),
            jax.ShapeDtypeStruct((GROUPS, ROWS), jnp.float32),
            jax.ShapeDtypeStruct((GROUPS, ROWS), jnp.float32),
        ),
        in_specs=[pl.BlockSpec(memory_space=pltpu.SMEM), vmem] + [any_space] * 10,
        out_specs=(vmem, vmem, vmem, vmem),
        scratch_shapes=[pltpu.SemaphoreType.DMA((32,))],
        compiler_params=pltpu.CompilerParams(vmem_limit_bytes=40 * 1024 * 1024),
        name="scores",
    )(place, centroids, *mine, *sibling)

    pair = jnp.stack([peak, total])
    top, amount = merge(spread(pair, ("z", "core"), 16))
    top, amount = merge(spread(jnp.stack([top, amount]), ("xl", "y", "xh"), 16))
    log_part = top + jnp.log2(amount)

    step = 256
    updated = pl.pallas_call(
        pull_kernel,
        grid=(kept // step,),
        out_shape=jax.ShapeDtypeStruct((kept, D), jnp.bfloat16),
        in_specs=[
            pl.BlockSpec((GROUPS, ROWS), lambda i: (0, 0)),
            pl.BlockSpec((step, D), lambda i: (i, 0)),
            pl.BlockSpec((GROUPS, 8, 2, 48, ROWS), lambda i: (0, 0, 0, 0, 0)),
            pl.BlockSpec((GROUPS, step, ROWS), lambda i: (0, i, 0)),
        ],
        out_specs=pl.BlockSpec((step, D), lambda i: (i, 0)),
        compiler_params=pltpu.CompilerParams(vmem_limit_bytes=40 * 1024 * 1024),
        name="pull",
    )(log_part, centroids, points_t, scores)

    own_rows = lax.dynamic_index_in_dim(
        log_part, my_y * 2 + lax.axis_index("xh"), 0, keepdims=False
    )
    return updated, own_rows * LN2


def solution(mesh):
    fine = Mesh(mesh.devices.reshape([SIZES[a] for a in AXES]), AXES)
    return jax.shard_map(
        per_device,
        mesh=fine,
        in_specs=(P(("y", "xh"), ("z", "xl", "core")), P(AXES, None)),
        out_specs=(P(AXES, None), P(("y", "xh"))),
        check_vma=False,
    )
```

```python
import functools
import itertools
import math

import jax
import jax.numpy as jnp
from jax import lax
from jax.experimental import pallas as pl
from jax.experimental.pallas import tpu as pltpu
from jax.sharding import Mesh
from jax.sharding import PartitionSpec as P

D = 768
AXES = ("z", "xl", "core", "y", "xh")
SIZES = {"z": 8, "xl": 2, "core": 2, "y": 4, "xh": 2}
LOG2E = math.log2(math.e)
LN2 = math.log(2.0)
SHARP2 = 4.0 / math.sqrt(D) * LOG2E
HALF = 128
ROWS = 256
GROUPS = 8


def permutation(move):
    places = list(itertools.product(*[range(SIZES[a]) for a in AXES]))
    number = {place: i for i, place in enumerate(places)}
    pairs = []
    for place in places:
        at = dict(zip(AXES, place))
        at["x"] = at["xh"] * 2 + at["xl"]
        src = move(at)
        src["xh"], src["xl"] = src["x"] // 2, src["x"] % 2
        pairs.append((number[tuple(src[a] for a in AXES)], number[place]))
    return pairs


def shifted(axis_of_core, step):
    def move(at):
        src = dict(at)
        axis = axis_of_core[at["core"]]
        src[axis] = (at[axis] + step) % 4
        return src

    return permutation(move)


def receive(value, pairs):
    return lax.ppermute(value, AXES, pairs)


FIRST = ("y", "x")
SECOND = ("x", "y")
SWAP = permutation(lambda at: {**at, "core": 1 - at["core"]})


AHEAD, BEHIND = 1, 3
PIECES = [
    [(0, k) for k in range(4)],
    [(AHEAD, 0), (AHEAD, 1), (BEHIND, 2), (BEHIND, 3), (AHEAD, 2), (AHEAD, 3), (BEHIND, 0), (BEHIND, 1)],
    [(2, k) for k in range(4)],
]


def rows_of(points_t, group):
    halves = [points_t[group, side].reshape(D, HALF) for side in range(2)]
    return jnp.concatenate(halves, axis=1)


def score_kernel(place, cents, *refs):
    pieces = refs[:6]
    points_t, scores, stat = refs[6:]
    core, my_x, my_y = place[0], place[1], place[2]
    for other in range(2):
        side = core if other == 0 else 1 - core
        for index, steps in enumerate(PIECES):
            for at, (second, first) in enumerate(steps):
                x = lax.rem(my_x + jnp.where(side == 0, second, first), 4)
                y = lax.rem(my_y + jnp.where(side == 0, first, second), 4)
                group = y * 2 + lax.div(x, 2)
                points_t[group, side, :, lax.rem(x, 2)] = pieces[other * 3 + index][at]
    part = cents.shape[0] // 2
    for group in range(GROUPS):
        block = rows_of(points_t, group)
        tops, totals = [], []
        for chunk in range(2):
            rows = pl.ds(chunk * part, part)
            value = jnp.dot(cents[rows, :], block, preferred_element_type=jnp.float32) * SHARP2
            top = jnp.max(value, axis=0, keepdims=True)
            scores[group, rows, :] = value
            tops.append(top)
            totals.append(jnp.sum(jnp.exp2(value - top), axis=0, keepdims=True))
        top = jnp.maximum(tops[0], tops[1])
        total = totals[0] * jnp.exp2(tops[0] - top) + totals[1] * jnp.exp2(tops[1] - top)
        stat[pl.ds(group, 1), :] = top + jnp.log2(total)


def merged(stats):
    values = [stats[i] for i in range(stats.shape[0])]
    top = functools.reduce(jnp.maximum, values)
    return top + jnp.log2(functools.reduce(jnp.add, [jnp.exp2(v - top) for v in values]))


def merge_kernel(stats, points_t, scores, stat, points_t_out, scores_out):
    stat[...] = merged(stats)


def pull_kernel(place, stats, cents, points_t, scores, out, own_rows, log_part):
    log_part[...] = merged(stats)
    own_rows[...] = log_part[pl.ds(place[2] * 2 + lax.div(place[1], 2), 1), :] * LN2
    acc = None
    mass = None
    for group in range(GROUPS):
        weights = jnp.exp2(scores[group] - log_part[pl.ds(group, 1), :]).astype(jnp.bfloat16)
        part = lax.dot_general(
            weights,
            rows_of(points_t, group),
            (((1,), (1,)), ((), ())),
            preferred_element_type=jnp.float32,
        )
        share = jnp.sum(weights.astype(jnp.float32), axis=1, keepdims=True)
        acc = part if acc is None else acc + part
        mass = share if mass is None else mass + share
    out[...] = ((cents[...].astype(jnp.float32) + acc) / (1.0 + mass)).astype(jnp.bfloat16)


def gather(points):
    feats = points.T
    halves = jnp.stack([feats[:, :HALF], feats[:, HALF:]])
    sent = jnp.broadcast_to(halves[None], (8,) + halves.shape).reshape((16,) + halves.shape[1:])
    block = lax.all_to_all(sent, ("z", "core"), 0, 0, tiled=True).reshape(8, 48, HALF)
    line = jnp.stack([block] + [receive(block, shifted(FIRST, k)) for k in (1, 2, 3)])
    ahead, behind = shifted(SECOND, 1), shifted(SECOND, 3)
    low, high = line[:2], line[2:]
    low_ahead, high_behind = receive(low, ahead), receive(high, behind)
    high_ahead, low_behind = receive(high, ahead), receive(low, behind)
    low_far, high_far = receive(low_ahead, ahead), receive(high_behind, behind)
    near = jnp.concatenate([low_ahead, high_behind, high_ahead, low_behind], axis=0)
    far = jnp.concatenate([low_far, high_far], axis=0)
    mine = [line, near, far]
    return mine + [receive(v, SWAP) for v in mine]


def spread(value, axes, count):
    copies = jnp.broadcast_to(value[None], (count,) + value.shape)
    return lax.all_to_all(copies, axes, 0, 0, tiled=True)


def kept_in_vmem(value):
    return pltpu.with_memory_space_constraint(value, pltpu.VMEM)


def per_device(points, centroids):
    kept = centroids.shape[0]
    my_y = lax.axis_index("y")
    my_x = lax.axis_index("xh") * 2 + lax.axis_index("xl")
    place = jnp.stack([lax.axis_index("core"), my_x, my_y]).astype(jnp.int32)
    pieces = gather(points)

    vmem = pl.BlockSpec(memory_space=pltpu.VMEM)
    smem = pl.BlockSpec(memory_space=pltpu.SMEM)
    params = pltpu.CompilerParams(vmem_limit_bytes=24 * 1024 * 1024)
    points_shape = pltpu.VMEM((GROUPS, 2, 8, 2, 48, HALF), jnp.bfloat16)
    scores_shape = pltpu.VMEM((GROUPS, kept, ROWS), jnp.float32)
    stat_shape = jax.ShapeDtypeStruct((GROUPS, ROWS), jnp.float32)
    points_t, scores, stat = pl.pallas_call(
        score_kernel,
        out_shape=(points_shape, scores_shape, stat_shape),
        in_specs=[smem] + [vmem] * 7,
        out_specs=(vmem,) * 3,
        compiler_params=params,
        name="scores",
    )(place, centroids, *pieces)

    stat, points_t, scores = pl.pallas_call(
        merge_kernel,
        out_shape=(stat_shape, points_shape, scores_shape),
        in_specs=[vmem] * 3,
        out_specs=(vmem,) * 3,
        input_output_aliases={1: 1, 2: 2},
        compiler_params=params,
        name="merge",
    )(spread(stat, ("z", "core"), 16), kept_in_vmem(points_t), kept_in_vmem(scores))

    updated, own_rows = pl.pallas_call(
        pull_kernel,
        out_shape=(
            jax.ShapeDtypeStruct((kept, D), jnp.bfloat16),
            jax.ShapeDtypeStruct((1, ROWS), jnp.float32),
        ),
        in_specs=[smem] + [vmem] * 4,
        out_specs=(vmem,) * 2,
        scratch_shapes=[pltpu.VMEM((GROUPS, ROWS), jnp.float32)],
        compiler_params=params,
        name="pull",
    )(
        place,
        spread(stat, ("xl", "y", "xh"), 16),
        centroids,
        kept_in_vmem(points_t),
        kept_in_vmem(scores),
    )
    return updated, own_rows.reshape(ROWS)


def solution(mesh):
    fine = Mesh(mesh.devices.reshape([SIZES[a] for a in AXES]), AXES)
    return jax.shard_map(
        per_device,
        mesh=fine,
        in_specs=(P(("y", "xh"), ("z", "xl", "core")), P(AXES, None)),
        out_specs=(P(AXES, None), P(("y", "xh"))),
        check_vma=False,
    )
```

```python
import functools
import itertools
import math

import jax
import jax.numpy as jnp
from jax import lax
from jax.experimental import pallas as pl
from jax.experimental.pallas import tpu as pltpu
from jax.sharding import Mesh
from jax.sharding import PartitionSpec as P

D = 768
AXES = ("z", "xl", "core", "y", "xh")
SIZES = {"z": 8, "xl": 2, "core": 2, "y": 4, "xh": 2}
LOG2E = math.log2(math.e)
LN2 = math.log(2.0)
SHARP2 = 4.0 / math.sqrt(D) * LOG2E
HALF = 128
ROWS = 256
GROUPS = 8
PAIRS = 4


def permutation(move):
    places = list(itertools.product(*[range(SIZES[a]) for a in AXES]))
    number = {place: i for i, place in enumerate(places)}
    pairs = []
    for place in places:
        at = dict(zip(AXES, place))
        at["x"] = at["xh"] * 2 + at["xl"]
        src = move(at)
        src["xh"], src["xl"] = src["x"] // 2, src["x"] % 2
        pairs.append((number[tuple(src[a] for a in AXES)], number[place]))
    return pairs


def shifted(axis_of_core, step):
    def move(at):
        src = dict(at)
        axis = axis_of_core[at["core"]]
        src[axis] = (at[axis] + step) % 4
        return src

    return permutation(move)


def receive(value, pairs):
    return lax.ppermute(value, AXES, pairs)


FIRST = ("x", "y")
SECOND = ("y", "x")
SWAP = permutation(lambda at: {**at, "core": 1 - at["core"]})


BLOCKS = [(second, first) for second in (0, 2, 1, 3) for first in range(4)]
CHUNKS = 4


def rows_of(points_t, pair):
    halves = [points_t[2 * pair + i].reshape(D, HALF) for i in range(2)]
    return jnp.concatenate(halves, axis=1)


def here():
    return lax.axis_index("core"), lax.axis_index("xh") * 2 + lax.axis_index("xl"), lax.axis_index("y")


def score_kernel(sibling, cents, blocks, points_t, scores, stat):
    core, my_x, my_y = here()
    side = 1 - core if sibling else core
    for at, (second, first) in enumerate(BLOCKS):
        x = lax.rem(my_x + jnp.where(side == 0, first, second), 4)
        y = lax.rem(my_y + jnp.where(side == 0, second, first), 4)
        points_t[y * 2 + lax.div(x, 2), :, lax.rem(x, 2)] = blocks[at]
    part = cents.shape[0] // CHUNKS
    for pair in range(PAIRS):
        block = rows_of(points_t, pair)
        tops, totals = [], []
        for chunk in range(CHUNKS):
            rows = pl.ds(chunk * part, part)
            value = jnp.dot(cents[rows, :], block, preferred_element_type=jnp.float32) * SHARP2
            top = jnp.max(value, axis=0, keepdims=True)
            scores[pair, rows, :] = value
            tops.append(top)
            totals.append(jnp.sum(jnp.exp2(value - top), axis=0, keepdims=True))
        top = functools.reduce(jnp.maximum, tops)
        total = functools.reduce(jnp.add, [s * jnp.exp2(t - top) for t, s in zip(tops, totals)])
        stat[pl.ds(pair, 1), :] = top + jnp.log2(total)


def merged(stats):
    values = [stats[i] for i in range(stats.shape[0])]
    top = functools.reduce(jnp.maximum, values)
    return top + jnp.log2(functools.reduce(jnp.add, [jnp.exp2(v - top) for v in values]))


def chip_kernel(mine, other, stat):
    core = lax.axis_index("core")
    sides = []
    for index in range(2):
        a = mine[index * PAIRS : (index + 1) * PAIRS, :]
        b = other[(1 - index) * PAIRS : (2 - index) * PAIRS, :]
        top = jnp.maximum(a, b)
        sides.append(top + jnp.log2(jnp.exp2(a - top) + jnp.exp2(b - top)))
    stat[:PAIRS, :] = jnp.where(core == 0, sides[0], sides[1])
    stat[PAIRS:, :] = jnp.where(core == 0, sides[1], sides[0])


def merge_kernel(stats, own_t, own_scores, sib_t, sib_scores, stat, *kept):
    stat[...] = merged(stats)


def pull_kernel(
    stats, cents, own_t, own_scores, sib_t, sib_scores, out, own_rows, log_part, block, sems
):
    core, my_x, my_y = here()
    log_part[...] = merged(stats)
    group = my_y * 2 + lax.div(my_x, 2)
    for side in range(2):
        pair = log_part[pl.ds(side * PAIRS + lax.div(group, 2), 1), :]
        half = jnp.where(lax.rem(group, 2) == 0, pair[:, :HALF], pair[:, HALF:])
        own_rows[:, side * HALF : (side + 1) * HALF] = half * LN2
    part = cents.shape[0] // CHUNKS
    copies = []
    for chunk in range(CHUNKS):
        rows = pl.ds(chunk * part, part)
        acc, mass = 0.0, 0.0
        for points_t, scores, side in ((own_t, own_scores, core), (sib_t, sib_scores, 1 - core)):
            for pair in range(PAIRS):
                log_rows = log_part[pl.ds(side * PAIRS + pair, 1), :]
                weights = jnp.exp2(scores[pair, rows, :] - log_rows).astype(jnp.bfloat16)
                acc = acc + lax.dot_general(
                    weights,
                    rows_of(points_t, pair),
                    (((1,), (1,)), ((), ())),
                    preferred_element_type=jnp.float32,
                )
                mass = mass + jnp.sum(weights.astype(jnp.float32), axis=1, keepdims=True)
        value = (cents[rows, :].astype(jnp.float32) + acc) / (1.0 + mass)
        block[rows, :] = value.astype(jnp.bfloat16)
        copies.append(pltpu.make_async_copy(block.at[rows], out.at[rows], sems.at[chunk]))
        copies[-1].start()
    for copy in copies:
        copy.wait()


def gather(points):
    feats = points.T
    halves = jnp.stack([feats[:, :HALF], feats[:, HALF:]])
    sent = jnp.broadcast_to(halves[None], (8,) + halves.shape).reshape((16,) + halves.shape[1:])
    block = lax.all_to_all(sent, ("z", "core"), 0, 0, tiled=True).reshape(8, 48, HALF)
    line = jnp.stack([block] + [receive(block, shifted(FIRST, k)) for k in (1, 2, 3)])
    return jnp.concatenate([line] + [receive(line, shifted(SECOND, k)) for k in (2, 1, 3)])


def spread(value, axes, count):
    copies = jnp.broadcast_to(value[None], (count,) + value.shape)
    return lax.all_to_all(copies, axes, 0, 0, tiled=True)


def kept_in_vmem(value):
    return pltpu.with_memory_space_constraint(value, pltpu.VMEM)


def per_device(points, centroids):
    kept = centroids.shape[0]
    vmem = pl.BlockSpec(memory_space=pltpu.VMEM)
    params = pltpu.CompilerParams(vmem_limit_bytes=24 * 1024 * 1024)
    points_shape = pltpu.VMEM((GROUPS, 8, 2, 48, HALF), jnp.bfloat16)
    scores_shape = pltpu.VMEM((PAIRS, kept, ROWS), jnp.float32)

    def score(blocks, sibling):
        return pl.pallas_call(
            functools.partial(score_kernel, sibling),
            out_shape=(
                points_shape,
                scores_shape,
                jax.ShapeDtypeStruct((PAIRS, ROWS), jnp.float32),
            ),
            in_specs=[vmem, vmem],
            out_specs=(vmem,) * 3,
            compiler_params=pltpu.CompilerParams(vmem_limit_bytes=12 * 1024 * 1024),
            name="sibling_scores" if sibling else "own_scores",
        )(centroids, kept_in_vmem(blocks))

    own = gather(points)
    swapped = receive(own, SWAP)
    own_t, own_scores, own_stat = score(own, False)
    sib_t, sib_scores, sib_stat = score(swapped, True)
    mine = jnp.concatenate([own_stat, sib_stat])
    stat = pl.pallas_call(
        chip_kernel,
        out_shape=jax.ShapeDtypeStruct((2 * PAIRS, ROWS), jnp.float32),
        in_specs=[vmem] * 2,
        out_specs=vmem,
        compiler_params=pltpu.CompilerParams(vmem_limit_bytes=2 * 1024 * 1024),
        name="chip",
    )(mine, receive(mine, SWAP))
    big = [own_t, own_scores, sib_t, sib_scores]

    stat, *big = pl.pallas_call(
        merge_kernel,
        out_shape=(
            jax.ShapeDtypeStruct((2 * PAIRS, ROWS), jnp.float32),
            points_shape,
            scores_shape,
            points_shape,
            scores_shape,
        ),
        in_specs=[vmem] * 5,
        out_specs=(vmem,) * 5,
        input_output_aliases={1: 1, 2: 2, 3: 3, 4: 4},
        compiler_params=params,
        name="merge",
    )(spread(stat, ("z",), 8), *[kept_in_vmem(v) for v in big])

    updated, own_rows = pl.pallas_call(
        pull_kernel,
        out_shape=(
            jax.ShapeDtypeStruct((kept, D), jnp.bfloat16),
            jax.ShapeDtypeStruct((1, ROWS), jnp.float32),
        ),
        in_specs=[vmem] * 6,
        out_specs=(pl.BlockSpec(memory_space=pl.ANY), vmem),
        scratch_shapes=[
            pltpu.VMEM((2 * PAIRS, ROWS), jnp.float32),
            pltpu.VMEM((kept, D), jnp.bfloat16),
            pltpu.SemaphoreType.DMA((CHUNKS,)),
        ],
        compiler_params=params,
        name="pull",
    )(spread(stat, ("xl", "y", "xh"), 16), centroids, *[kept_in_vmem(v) for v in big])
    return updated, own_rows.reshape(ROWS)


def solution(mesh):
    fine = Mesh(mesh.devices.reshape([SIZES[a] for a in AXES]), AXES)
    return jax.shard_map(
        per_device,
        mesh=fine,
        in_specs=(P(("y", "xh"), ("z", "xl", "core")), P(AXES, None)),
        out_specs=(P(AXES, None), P(("y", "xh"))),
        check_vma=False,
    )
```

```python
import functools
import itertools
import math

import jax
import jax.numpy as jnp
from jax import lax
from jax.experimental import pallas as pl
from jax.experimental.pallas import tpu as pltpu
from jax.sharding import Mesh
from jax.sharding import PartitionSpec as P

D = 768
AXES = ("z", "xl", "core", "y", "xh")
SIZES = {"z": 8, "xl": 2, "core": 2, "y": 4, "xh": 2}
LOG2E = math.log2(math.e)
LN2 = math.log(2.0)
SHARP2 = 4.0 / math.sqrt(D) * LOG2E
HALF = 128
ROWS = 256
GROUPS = 8
PAIRS = 4


def permutation(move):
    places = list(itertools.product(*[range(SIZES[a]) for a in AXES]))
    number = {place: i for i, place in enumerate(places)}
    pairs = []
    for place in places:
        at = dict(zip(AXES, place))
        at["x"] = at["xh"] * 2 + at["xl"]
        src = move(at)
        src["xh"], src["xl"] = src["x"] // 2, src["x"] % 2
        pairs.append((number[tuple(src[a] for a in AXES)], number[place]))
    return pairs


def shifted(axis_of_core, step):
    def move(at):
        src = dict(at)
        axis = axis_of_core[at["core"]]
        src[axis] = (at[axis] + step) % 4
        return src

    return permutation(move)


def receive(value, pairs):
    return lax.ppermute(value, AXES, pairs)


FIRST = ("x", "y")
SECOND = ("y", "x")
SWAP = permutation(lambda at: {**at, "core": 1 - at["core"]})


BLOCKS = [
    (second, first) for firsts in ((0, 1), (3, 2)) for second in (0, 2, 1, 3) for first in firsts
]
CHUNKS = 4


def rows_of(points_t, pair):
    halves = [points_t[2 * pair + i].reshape(D, HALF) for i in range(2)]
    return jnp.concatenate(halves, axis=1)


def here():
    return lax.axis_index("core"), lax.axis_index("xh") * 2 + lax.axis_index("xl"), lax.axis_index("y")


def score_kernel(sibling, cents, blocks, points_t, scores, stat):
    core, my_x, my_y = here()
    side = 1 - core if sibling else core
    for at, (second, first) in enumerate(BLOCKS):
        x = lax.rem(my_x + jnp.where(side == 0, first, second), 4)
        y = lax.rem(my_y + jnp.where(side == 0, second, first), 4)
        points_t[y * 2 + lax.div(x, 2), :, lax.rem(x, 2)] = blocks[at]
    part = cents.shape[0] // CHUNKS
    for pair in range(PAIRS):
        block = rows_of(points_t, pair)
        tops, totals = [], []
        for chunk in range(CHUNKS):
            rows = pl.ds(chunk * part, part)
            value = jnp.dot(cents[rows, :], block, preferred_element_type=jnp.float32) * SHARP2
            top = jnp.max(value, axis=0, keepdims=True)
            scores[pair, rows, :] = value
            tops.append(top)
            totals.append(jnp.sum(jnp.exp2(value - top), axis=0, keepdims=True))
        top = functools.reduce(jnp.maximum, tops)
        total = functools.reduce(jnp.add, [s * jnp.exp2(t - top) for t, s in zip(tops, totals)])
        stat[pl.ds(pair, 1), :] = top + jnp.log2(total)


def merged(stats):
    values = [stats[i] for i in range(stats.shape[0])]
    top = functools.reduce(jnp.maximum, values)
    return top + jnp.log2(functools.reduce(jnp.add, [jnp.exp2(v - top) for v in values]))


def chip_kernel(mine, other, stat):
    core = lax.axis_index("core")
    sides = []
    for index in range(2):
        a = mine[index * PAIRS : (index + 1) * PAIRS, :]
        b = other[(1 - index) * PAIRS : (2 - index) * PAIRS, :]
        top = jnp.maximum(a, b)
        sides.append(top + jnp.log2(jnp.exp2(a - top) + jnp.exp2(b - top)))
    stat[:PAIRS, :] = jnp.where(core == 0, sides[0], sides[1])
    stat[PAIRS:, :] = jnp.where(core == 0, sides[1], sides[0])


def merge_kernel(stats, own_t, own_scores, sib_t, sib_scores, stat, *kept):
    stat[...] = merged(stats)


def pull_kernel(
    stats, cents, own_t, own_scores, sib_t, sib_scores, out, own_rows, log_part, block, sems
):
    core, my_x, my_y = here()
    log_part[...] = merged(stats)
    group = my_y * 2 + lax.div(my_x, 2)
    for side in range(2):
        pair = log_part[pl.ds(side * PAIRS + lax.div(group, 2), 1), :]
        half = jnp.where(lax.rem(group, 2) == 0, pair[:, :HALF], pair[:, HALF:])
        own_rows[:, side * HALF : (side + 1) * HALF] = half * LN2
    part = cents.shape[0] // CHUNKS
    copies = []
    for chunk in range(CHUNKS):
        rows = pl.ds(chunk * part, part)
        acc, mass = 0.0, 0.0
        for points_t, scores, side in ((own_t, own_scores, core), (sib_t, sib_scores, 1 - core)):
            for pair in range(PAIRS):
                log_rows = log_part[pl.ds(side * PAIRS + pair, 1), :]
                weights = jnp.exp2(scores[pair, rows, :] - log_rows).astype(jnp.bfloat16)
                acc = acc + lax.dot_general(
                    weights,
                    rows_of(points_t, pair),
                    (((1,), (1,)), ((), ())),
                    preferred_element_type=jnp.float32,
                )
                mass = mass + jnp.sum(weights.astype(jnp.float32), axis=1, keepdims=True)
        value = (cents[rows, :].astype(jnp.float32) + acc) / (1.0 + mass)
        block[rows, :] = value.astype(jnp.bfloat16)
        copies.append(pltpu.make_async_copy(block.at[rows], out.at[rows], sems.at[chunk]))
        copies[-1].start()
    for copy in copies:
        copy.wait()


def gather(points):
    feats = points.T
    halves = jnp.stack([feats[:, :HALF], feats[:, HALF:]])
    sent = jnp.broadcast_to(halves[None], (8,) + halves.shape).reshape((16,) + halves.shape[1:])
    block = lax.all_to_all(sent, ("z", "core"), 0, 0, tiled=True).reshape(8, 48, HALF)
    ahead, far, behind = [receive(block, shifted(FIRST, k)) for k in (1, 2, 3)]
    own = []
    for couple in ([block, ahead], [behind, far]):
        couple = jnp.stack(couple)
        own += [couple] + [receive(couple, shifted(SECOND, k)) for k in (2, 1, 3)]
    return jnp.concatenate(lax.optimization_barrier(own))


def spread(value, axes, count):
    copies = jnp.broadcast_to(value[None], (count,) + value.shape)
    return lax.all_to_all(copies, axes, 0, 0, tiled=True)


def kept_in_vmem(value):
    return pltpu.with_memory_space_constraint(value, pltpu.VMEM)


def per_device(points, centroids):
    kept = centroids.shape[0]
    vmem = pl.BlockSpec(memory_space=pltpu.VMEM)
    params = pltpu.CompilerParams(vmem_limit_bytes=24 * 1024 * 1024)
    points_shape = pltpu.VMEM((GROUPS, 8, 2, 48, HALF), jnp.bfloat16)
    scores_shape = pltpu.VMEM((PAIRS, kept, ROWS), jnp.float32)

    def score(blocks, sibling):
        return pl.pallas_call(
            functools.partial(score_kernel, sibling),
            out_shape=(
                points_shape,
                scores_shape,
                jax.ShapeDtypeStruct((PAIRS, ROWS), jnp.float32),
            ),
            in_specs=[vmem, vmem],
            out_specs=(vmem,) * 3,
            compiler_params=pltpu.CompilerParams(vmem_limit_bytes=12 * 1024 * 1024),
            name="sibling_scores" if sibling else "own_scores",
        )(centroids, kept_in_vmem(blocks))

    own = gather(points)
    swapped = receive(own, SWAP)
    own_t, own_scores, own_stat = score(own, False)
    sib_t, sib_scores, sib_stat = score(swapped, True)
    mine = jnp.concatenate([own_stat, sib_stat])
    stat = pl.pallas_call(
        chip_kernel,
        out_shape=jax.ShapeDtypeStruct((2 * PAIRS, ROWS), jnp.float32),
        in_specs=[vmem] * 2,
        out_specs=vmem,
        compiler_params=pltpu.CompilerParams(vmem_limit_bytes=2 * 1024 * 1024),
        name="chip",
    )(mine, receive(mine, SWAP))
    big = [own_t, own_scores, sib_t, sib_scores]

    stat, *big = pl.pallas_call(
        merge_kernel,
        out_shape=(
            jax.ShapeDtypeStruct((2 * PAIRS, ROWS), jnp.float32),
            points_shape,
            scores_shape,
            points_shape,
            scores_shape,
        ),
        in_specs=[vmem] * 5,
        out_specs=(vmem,) * 5,
        input_output_aliases={1: 1, 2: 2, 3: 3, 4: 4},
        compiler_params=params,
        name="merge",
    )(spread(stat, ("z",), 8), *[kept_in_vmem(v) for v in big])

    updated, own_rows = pl.pallas_call(
        pull_kernel,
        out_shape=(
            jax.ShapeDtypeStruct((kept, D), jnp.bfloat16),
            jax.ShapeDtypeStruct((1, ROWS), jnp.float32),
        ),
        in_specs=[vmem] * 6,
        out_specs=(pl.BlockSpec(memory_space=pl.ANY), vmem),
        scratch_shapes=[
            pltpu.VMEM((2 * PAIRS, ROWS), jnp.float32),
            pltpu.VMEM((kept, D), jnp.bfloat16),
            pltpu.SemaphoreType.DMA((CHUNKS,)),
        ],
        compiler_params=params,
        name="pull",
    )(spread(stat, ("xl", "y", "xh"), 16), centroids, *[kept_in_vmem(v) for v in big])
    return updated, own_rows.reshape(ROWS)


def solution(mesh):
    fine = Mesh(mesh.devices.reshape([SIZES[a] for a in AXES]), AXES)
    return jax.shard_map(
        per_device,
        mesh=fine,
        in_specs=(P(("y", "xh"), ("z", "xl", "core")), P(AXES, None)),
        out_specs=(P(AXES, None), P(("y", "xh"))),
        check_vma=False,
    )
```

```python
import functools
import itertools
import math

import jax
import jax.numpy as jnp
from jax import lax
from jax.experimental import pallas as pl
from jax.experimental.pallas import tpu as pltpu
from jax.sharding import Mesh
from jax.sharding import PartitionSpec as P

D = 768
AXES = ("z", "xl", "core", "y", "xh")
SIZES = {"z": 8, "xl": 2, "core": 2, "y": 4, "xh": 2}
LOG2E = math.log2(math.e)
LN2 = math.log(2.0)
SHARP2 = 4.0 / math.sqrt(D) * LOG2E
HALF = 128
ROWS = 256
GROUPS = 8
PAIRS = 4


def permutation(move):
    places = list(itertools.product(*[range(SIZES[a]) for a in AXES]))
    number = {place: i for i, place in enumerate(places)}
    pairs = []
    for place in places:
        at = dict(zip(AXES, place))
        at["x"] = at["xh"] * 2 + at["xl"]
        src = move(at)
        src["xh"], src["xl"] = src["x"] // 2, src["x"] % 2
        pairs.append((number[tuple(src[a] for a in AXES)], number[place]))
    return pairs


def shifted(axis_of_core, step):
    def move(at):
        src = dict(at)
        axis = axis_of_core[at["core"]]
        src[axis] = (at[axis] + step) % 4
        return src

    return permutation(move)


def receive(value, pairs):
    return lax.ppermute(value, AXES, pairs)


FIRST = ("x", "y")
SECOND = ("y", "x")
SWAP = permutation(lambda at: {**at, "core": 1 - at["core"]})


STEPS = ((2, 1, 3), (1, 3, 2))
BLOCKS = [
    (second, first)
    for firsts, steps in zip(((0, 1), (3, 2)), STEPS)
    for second in (0, *steps)
    for first in firsts
]
CHUNKS = 4


def rows_of(points_t, pair):
    halves = [points_t[2 * pair + i].reshape(D, HALF) for i in range(2)]
    return jnp.concatenate(halves, axis=1)


def here():
    return lax.axis_index("core"), lax.axis_index("xh") * 2 + lax.axis_index("xl"), lax.axis_index("y")


def score_kernel(sibling, cents, early, late, points_t, scores, stat):
    core, my_x, my_y = here()
    side = 1 - core if sibling else core
    for at, (second, first) in enumerate(BLOCKS):
        x = lax.rem(my_x + jnp.where(side == 0, first, second), 4)
        y = lax.rem(my_y + jnp.where(side == 0, second, first), 4)
        points_t[y * 2 + lax.div(x, 2), :, lax.rem(x, 2)] = early[at] if at < 8 else late[at - 8]
    part = cents.shape[0] // CHUNKS
    for pair in range(PAIRS):
        block = rows_of(points_t, pair)
        tops, totals = [], []
        for chunk in range(CHUNKS):
            rows = pl.ds(chunk * part, part)
            value = jnp.dot(cents[rows, :], block, preferred_element_type=jnp.float32) * SHARP2
            top = jnp.max(value, axis=0, keepdims=True)
            scores[pair, rows, :] = value
            tops.append(top)
            totals.append(jnp.sum(jnp.exp2(value - top), axis=0, keepdims=True))
        top = functools.reduce(jnp.maximum, tops)
        total = functools.reduce(jnp.add, [s * jnp.exp2(t - top) for t, s in zip(tops, totals)])
        stat[pl.ds(pair, 1), :] = top + jnp.log2(total)


def merged(stats):
    values = [stats[i] for i in range(stats.shape[0])]
    top = functools.reduce(jnp.maximum, values)
    return top + jnp.log2(functools.reduce(jnp.add, [jnp.exp2(v - top) for v in values]))


def chip_kernel(mine, other, stat):
    core = lax.axis_index("core")
    sides = []
    for index in range(2):
        a = mine[index * PAIRS : (index + 1) * PAIRS, :]
        b = other[(1 - index) * PAIRS : (2 - index) * PAIRS, :]
        top = jnp.maximum(a, b)
        sides.append(top + jnp.log2(jnp.exp2(a - top) + jnp.exp2(b - top)))
    stat[:PAIRS, :] = jnp.where(core == 0, sides[0], sides[1])
    stat[PAIRS:, :] = jnp.where(core == 0, sides[1], sides[0])


def merge_kernel(stats, own_t, own_scores, sib_t, sib_scores, stat, *kept):
    stat[...] = merged(stats)


def pull_kernel(
    stats, cents, own_t, own_scores, sib_t, sib_scores, out, own_rows, log_part, block, sems
):
    core, my_x, my_y = here()
    log_part[...] = merged(stats)
    group = my_y * 2 + lax.div(my_x, 2)
    for side in range(2):
        pair = log_part[pl.ds(side * PAIRS + lax.div(group, 2), 1), :]
        half = jnp.where(lax.rem(group, 2) == 0, pair[:, :HALF], pair[:, HALF:])
        own_rows[:, side * HALF : (side + 1) * HALF] = half * LN2
    part = cents.shape[0] // CHUNKS
    copies = []
    for chunk in range(CHUNKS):
        rows = pl.ds(chunk * part, part)
        acc, mass = 0.0, 0.0
        for points_t, scores, side in ((own_t, own_scores, core), (sib_t, sib_scores, 1 - core)):
            for pair in range(PAIRS):
                log_rows = log_part[pl.ds(side * PAIRS + pair, 1), :]
                weights = jnp.exp2(scores[pair, rows, :] - log_rows).astype(jnp.bfloat16)
                acc = acc + lax.dot_general(
                    weights,
                    rows_of(points_t, pair),
                    (((1,), (1,)), ((), ())),
                    preferred_element_type=jnp.float32,
                )
                mass = mass + jnp.sum(weights.astype(jnp.float32), axis=1, keepdims=True)
        value = (cents[rows, :].astype(jnp.float32) + acc) / (1.0 + mass)
        block[rows, :] = value.astype(jnp.bfloat16)
        copies.append(pltpu.make_async_copy(block.at[rows], out.at[rows], sems.at[chunk]))
        copies[-1].start()
    for copy in copies:
        copy.wait()


def gather(points):
    feats = points.T
    halves = jnp.stack([feats[:, :HALF], feats[:, HALF:]])
    sent = jnp.broadcast_to(halves[None], (8,) + halves.shape).reshape((16,) + halves.shape[1:])
    block = lax.all_to_all(sent, ("z", "core"), 0, 0, tiled=True).reshape(8, 48, HALF)
    ahead, far, behind = [receive(block, shifted(FIRST, k)) for k in (1, 2, 3)]
    own = []
    for couple, steps in (([block, ahead], STEPS[0]), ([behind, far], STEPS[1])):
        couple = jnp.stack(couple)
        own += [couple] + [receive(couple, shifted(SECOND, k)) for k in steps]
    own = lax.optimization_barrier(own)
    return [jnp.concatenate(own[:4]), jnp.concatenate(own[4:])]


def spread(value, axes, count):
    copies = jnp.broadcast_to(value[None], (count,) + value.shape)
    return lax.all_to_all(copies, axes, 0, 0, tiled=True)


def kept_in_vmem(value):
    return pltpu.with_memory_space_constraint(value, pltpu.VMEM)


def per_device(points, centroids):
    kept = centroids.shape[0]
    vmem = pl.BlockSpec(memory_space=pltpu.VMEM)
    params = pltpu.CompilerParams(vmem_limit_bytes=24 * 1024 * 1024)
    points_shape = pltpu.VMEM((GROUPS, 8, 2, 48, HALF), jnp.bfloat16)
    scores_shape = pltpu.VMEM((PAIRS, kept, ROWS), jnp.float32)

    def score(blocks, sibling):
        return pl.pallas_call(
            functools.partial(score_kernel, sibling),
            out_shape=(
                points_shape,
                scores_shape,
                jax.ShapeDtypeStruct((PAIRS, ROWS), jnp.float32),
            ),
            in_specs=[vmem] * 3,
            out_specs=(vmem,) * 3,
            compiler_params=pltpu.CompilerParams(vmem_limit_bytes=12 * 1024 * 1024),
            name="sibling_scores" if sibling else "own_scores",
        )(centroids, *[kept_in_vmem(v) for v in blocks])

    own = gather(points)
    swapped = [receive(v, SWAP) for v in own]
    own_t, own_scores, own_stat = score(own, False)
    sib_t, sib_scores, sib_stat = score(swapped, True)
    mine = jnp.concatenate([own_stat, sib_stat])
    stat = pl.pallas_call(
        chip_kernel,
        out_shape=jax.ShapeDtypeStruct((2 * PAIRS, ROWS), jnp.float32),
        in_specs=[vmem] * 2,
        out_specs=vmem,
        compiler_params=pltpu.CompilerParams(vmem_limit_bytes=2 * 1024 * 1024),
        name="chip",
    )(mine, receive(mine, SWAP))
    big = [own_t, own_scores, sib_t, sib_scores]

    stat, *big = pl.pallas_call(
        merge_kernel,
        out_shape=(
            jax.ShapeDtypeStruct((2 * PAIRS, ROWS), jnp.float32),
            points_shape,
            scores_shape,
            points_shape,
            scores_shape,
        ),
        in_specs=[vmem] * 5,
        out_specs=(vmem,) * 5,
        input_output_aliases={1: 1, 2: 2, 3: 3, 4: 4},
        compiler_params=params,
        name="merge",
    )(spread(stat, ("z",), 8), *[kept_in_vmem(v) for v in big])

    updated, own_rows = pl.pallas_call(
        pull_kernel,
        out_shape=(
            jax.ShapeDtypeStruct((kept, D), jnp.bfloat16),
            jax.ShapeDtypeStruct((1, ROWS), jnp.float32),
        ),
        in_specs=[vmem] * 6,
        out_specs=(pl.BlockSpec(memory_space=pl.ANY), vmem),
        scratch_shapes=[
            pltpu.VMEM((2 * PAIRS, ROWS), jnp.float32),
            pltpu.VMEM((kept, D), jnp.bfloat16),
            pltpu.SemaphoreType.DMA((CHUNKS,)),
        ],
        compiler_params=params,
        name="pull",
    )(spread(stat, ("y", "xh", "xl"), 16), centroids, *[kept_in_vmem(v) for v in big])
    return updated, own_rows.reshape(ROWS)


def solution(mesh):
    fine = Mesh(mesh.devices.reshape([SIZES[a] for a in AXES]), AXES)
    return jax.shard_map(
        per_device,
        mesh=fine,
        in_specs=(P(("y", "xh"), ("z", "xl", "core")), P(AXES, None)),
        out_specs=(P(AXES, None), P(("y", "xh"))),
        check_vma=False,
    )
```

```python
import functools
import itertools
import math

import jax
import jax.numpy as jnp
from jax import lax
from jax.experimental import pallas as pl
from jax.experimental.pallas import tpu as pltpu
from jax.sharding import Mesh
from jax.sharding import PartitionSpec as P

D = 768
AXES = ("z", "xl", "core", "y", "xh")
SIZES = {"z": 8, "xl": 2, "core": 2, "y": 4, "xh": 2}
LOG2E = math.log2(math.e)
LN2 = math.log(2.0)
SHARP2 = 4.0 / math.sqrt(D) * LOG2E
HALF = 128
ROWS = 256
GROUPS = 8


def permutation(move):
    places = list(itertools.product(*[range(SIZES[a]) for a in AXES]))
    number = {place: i for i, place in enumerate(places)}
    pairs = []
    for place in places:
        at = dict(zip(AXES, place))
        at["x"] = at["xh"] * 2 + at["xl"]
        src = move(at)
        src["xh"], src["xl"] = src["x"] // 2, src["x"] % 2
        pairs.append((number[tuple(src[a] for a in AXES)], number[place]))
    return pairs


def crossed(axis_of_core, step):
    def move(at):
        axis = axis_of_core[at["core"]]
        return {**at, axis: at[axis] ^ step}

    return permutation(move)


def shifted(axis_of_core, step):
    def move(at):
        axis = axis_of_core[at["core"]]
        return {**at, axis: (at[axis] + step) % 4}

    return permutation(move)


def receive(value, pairs):
    return lax.ppermute(value, AXES, pairs)


FIRST = ("x", "y")
SECOND = ("y", "x")
SWAP = permutation(lambda at: {**at, "core": 1 - at["core"]})


STEPS = ((2, 1, 3), (1, 3, 2))
BLOCKS = [
    [(second, which) for second in (0, *steps) for which in range(2)] for steps in STEPS
]
UNITS = 4
CHUNKS = 4
COUPLES = [(sibling, couple) for sibling in range(2) for couple in range(2)]


def rows_of(points_t, pair):
    halves = [points_t[2 * pair + i].reshape(D, HALF) for i in range(2)]
    return jnp.concatenate(halves, axis=1)


def here():
    return lax.axis_index("core"), lax.axis_index("xh") * 2 + lax.axis_index("xl"), lax.axis_index("y")


def row_of(sibling, couple, unit):
    core, my_x, my_y = here()
    side = 1 - core if sibling else core
    my_half = lax.div(my_x, 2)
    along_y = unit * 2 + (my_half ^ couple)
    along_x = (my_y ^ (2 * couple + unit // 2)) * 2 + unit % 2
    return side * GROUPS + jnp.where(side == 0, along_y, along_x)


def score_kernel(sibling, couple, cents, blocks, *refs):
    points_t, scores, stat = refs[-3:]
    core, my_x, my_y = here()
    side = 1 - core if sibling else core
    for at, (second, which) in enumerate(BLOCKS[couple]):
        x, y = lax.rem(my_x + second, 4), lax.rem(my_y + second, 4)
        unit = jnp.where(side == 0, y, which * 2 + lax.div(x, 2))
        low = jnp.where(side == 0, lax.rem(my_x, 2) ^ which, lax.rem(x, 2))
        points_t[unit, :, low] = blocks[at]
    part = cents.shape[0] // CHUNKS
    logs = []
    for pair in range(UNITS // 2):
        block = rows_of(points_t, pair)
        tops, totals = [], []
        for chunk in range(CHUNKS):
            rows = pl.ds(chunk * part, part)
            value = jnp.dot(cents[rows, :], block, preferred_element_type=jnp.float32) * SHARP2
            top = jnp.max(value, axis=0, keepdims=True)
            scores[pair, rows, :] = value
            tops.append(top)
            totals.append(jnp.sum(jnp.exp2(value - top), axis=0, keepdims=True))
        top = functools.reduce(jnp.maximum, tops)
        total = sum(s * jnp.exp2(t - top) for t, s in zip(tops, totals))
        log = top + jnp.log2(total)
        logs += [log[:, :HALF], log[:, HALF:]]
    if (sibling, couple) != COUPLES[-1]:
        stat[...] = jnp.concatenate(logs, axis=0)
        return
    parts = [[ref[pl.ds(u, 1), :] for u in range(UNITS)] for ref in refs[:-3]] + [logs]
    for (other, second_couple), values in zip(COUPLES, parts):
        for unit, value in enumerate(values):
            stat[pl.ds(row_of(other, second_couple, unit), 1), :] = value


def merged(stats):
    values = [stats[i] for i in range(stats.shape[0])]
    top = functools.reduce(jnp.maximum, values)
    return top + jnp.log2(functools.reduce(jnp.add, [jnp.exp2(v - top) for v in values]))


def chip_kernel(mine, other, stat):
    core = lax.axis_index("core")
    a = jnp.where(core == 0, mine[...], other[...])
    b = jnp.where(core == 0, other[...], mine[...])
    top = jnp.maximum(a, b)
    stat[...] = top + jnp.log2(jnp.exp2(a - top) + jnp.exp2(b - top))


def merge_kernel(stats, *refs):
    refs[len(refs) // 2][...] = merged(stats)


def pull_kernel(stats, cents, *refs):
    big, (out, own_rows, log_part, block, sems) = refs[:-5], refs[-5:]
    core, my_x, my_y = here()
    log_part[...] = merged(stats)
    group = my_y * 2 + lax.div(my_x, 2)
    for side in range(2):
        half = log_part[pl.ds(side * GROUPS + group, 1), :]
        own_rows[:, side * HALF : (side + 1) * HALF] = half * LN2
    work = []
    for index, (sibling, couple) in enumerate(COUPLES):
        for pair in range(UNITS // 2):
            logs = [log_part[pl.ds(row_of(sibling, couple, 2 * pair + i), 1), :] for i in range(2)]
            work.append((big[2 * index], big[2 * index + 1], pair, jnp.concatenate(logs, axis=1)))
    part = cents.shape[0] // CHUNKS
    copies = []
    for chunk in range(CHUNKS):
        rows = pl.ds(chunk * part, part)
        acc, mass = 0.0, 0.0
        for points_t, scores, pair, log_rows in work:
            weights = jnp.exp2(scores[pair, rows, :] - log_rows).astype(jnp.bfloat16)
            acc = acc + lax.dot_general(
                weights,
                rows_of(points_t, pair),
                (((1,), (1,)), ((), ())),
                preferred_element_type=jnp.float32,
            )
            mass = mass + jnp.sum(weights.astype(jnp.float32), axis=1, keepdims=True)
        value = (cents[rows, :].astype(jnp.float32) + acc) / (1.0 + mass)
        block[rows, :] = value.astype(jnp.bfloat16)
        copies.append(pltpu.make_async_copy(block.at[rows], out.at[rows], sems.at[chunk]))
        copies[-1].start()
    for copy in copies:
        copy.wait()


def gather(points):
    feats = points.T
    halves = jnp.stack([feats[:, :HALF], feats[:, HALF:]])
    sent = jnp.broadcast_to(halves[None], (8,) + halves.shape).reshape((16,) + halves.shape[1:])
    block = lax.all_to_all(sent, ("z", "core"), 0, 0, tiled=True).reshape(8, 48, HALF)
    one, two, three = [receive(block, crossed(FIRST, k)) for k in (1, 2, 3)]
    couples = []
    for couple, steps in zip(([block, one], [two, three]), STEPS):
        couple = jnp.stack(couple)
        pieces = [couple] + [receive(couple, shifted(SECOND, k)) for k in steps]
        couples.append(pieces)
    return [jnp.concatenate(pieces) for pieces in lax.optimization_barrier(couples)]


def spread(value, axes, count):
    copies = jnp.broadcast_to(value[None], (count,) + value.shape)
    return lax.all_to_all(copies, axes, 0, 0, tiled=True)


def kept_in_vmem(value):
    return pltpu.with_memory_space_constraint(value, pltpu.VMEM)


def limit(megabytes):
    return pltpu.CompilerParams(vmem_limit_bytes=megabytes * 1024 * 1024)


def per_device(points, centroids):
    kept = centroids.shape[0]
    vmem = pl.BlockSpec(memory_space=pltpu.VMEM)
    points_shape = pltpu.VMEM((UNITS, 8, 2, 48, HALF), jnp.bfloat16)
    scores_shape = pltpu.VMEM((UNITS // 2, kept, ROWS), jnp.float32)
    stat_shape = jax.ShapeDtypeStruct((2 * GROUPS, HALF), jnp.float32)
    unit_shape = jax.ShapeDtypeStruct((UNITS, HALF), jnp.float32)

    big, stats = [], []
    own = gather(points)
    for sibling, couple in COUPLES:
        blocks = receive(own[couple], SWAP) if sibling else own[couple]
        last = (sibling, couple) == COUPLES[-1]
        earlier = stats if last else []
        points_t, scores, stat = pl.pallas_call(
            functools.partial(score_kernel, sibling, couple),
            out_shape=(points_shape, scores_shape, stat_shape if last else unit_shape),
            in_specs=[vmem] * (2 + len(earlier)),
            out_specs=(vmem,) * 3,
            compiler_params=limit(12),
            name=("sibling" if sibling else "own") + str(couple),
        )(centroids, kept_in_vmem(blocks), *earlier)
        big += [points_t, scores]
        stats.append(stat)

    mine = stats[-1]
    stat = pl.pallas_call(
        chip_kernel,
        out_shape=stat_shape,
        in_specs=[vmem] * 2,
        out_specs=vmem,
        compiler_params=limit(2),
        name="chip",
    )(mine, receive(mine, SWAP))

    shapes = [points_shape, scores_shape] * len(COUPLES)
    stat, *big = pl.pallas_call(
        merge_kernel,
        out_shape=(stat_shape, *shapes),
        in_specs=[vmem] * (1 + len(big)),
        out_specs=(vmem,) * (1 + len(big)),
        input_output_aliases={i: i for i in range(1, 1 + len(big))},
        compiler_params=limit(24),
        name="merge",
    )(spread(stat, ("z",), 8), *[kept_in_vmem(v) for v in big])

    updated, own_rows = pl.pallas_call(
        pull_kernel,
        out_shape=(
            jax.ShapeDtypeStruct((kept, D), jnp.bfloat16),
            jax.ShapeDtypeStruct((1, ROWS), jnp.float32),
        ),
        in_specs=[vmem] * (2 + len(big)),
        out_specs=(pl.BlockSpec(memory_space=pl.ANY), vmem),
        scratch_shapes=[
            pltpu.VMEM((2 * GROUPS, HALF), jnp.float32),
            pltpu.VMEM((kept, D), jnp.bfloat16),
            pltpu.SemaphoreType.DMA((CHUNKS,)),
        ],
        compiler_params=limit(24),
        name="pull",
    )(spread(stat, ("xl", "y", "xh"), 16), centroids, *[kept_in_vmem(v) for v in big])
    return updated, own_rows.reshape(ROWS)


def solution(mesh):
    fine = Mesh(mesh.devices.reshape([SIZES[a] for a in AXES]), AXES)
    return jax.shard_map(
        per_device,
        mesh=fine,
        in_specs=(P(("y", "xh"), ("z", "xl", "core")), P(AXES, None)),
        out_specs=(P(AXES, None), P(("y", "xh"))),
        check_vma=False,
    )
```

```python
import functools
import itertools
import math

import jax
import jax.numpy as jnp
from jax import lax
from jax.experimental import pallas as pl
from jax.experimental.pallas import tpu as pltpu
from jax.sharding import Mesh
from jax.sharding import PartitionSpec as P

D = 768
AXES = ("z", "xl", "core", "y", "xh")
SIZES = {"z": 8, "xl": 2, "core": 2, "y": 4, "xh": 2}
LOG2E = math.log2(math.e)
LN2 = math.log(2.0)
SHARP2 = 4.0 / math.sqrt(D) * LOG2E
HALF = 128
ROWS = 256
GROUPS = 8


def permutation(move):
    places = list(itertools.product(*[range(SIZES[a]) for a in AXES]))
    number = {place: i for i, place in enumerate(places)}
    pairs = []
    for place in places:
        at = dict(zip(AXES, place))
        at["x"] = at["xh"] * 2 + at["xl"]
        src = move(at)
        src["xh"], src["xl"] = src["x"] // 2, src["x"] % 2
        pairs.append((number[tuple(src[a] for a in AXES)], number[place]))
    return pairs


def crossed(axis_of_core, step):
    def move(at):
        axis = axis_of_core[at["core"]]
        return {**at, axis: at[axis] ^ step}

    return permutation(move)


def shifted(axis_of_core, step):
    def move(at):
        axis = axis_of_core[at["core"]]
        return {**at, axis: (at[axis] + step) % 4}

    return permutation(move)


def receive(value, pairs):
    return lax.ppermute(value, AXES, pairs)


FIRST = ("x", "y")
SECOND = ("y", "x")
SWAP = permutation(lambda at: {**at, "core": 1 - at["core"]})


STEPS = ((2, 1, 3), (2, 1, 3))
BLOCKS = [
    [(second, which) for second in (0, *steps) for which in range(2)] for steps in STEPS
]
UNITS = 4
CHUNKS = 4
COUPLES = [(sibling, couple) for sibling in range(2) for couple in range(2)]


def rows_of(points_t, pair):
    halves = [points_t[2 * pair + i].reshape(D, HALF) for i in range(2)]
    return jnp.concatenate(halves, axis=1)


def here():
    return lax.axis_index("core"), lax.axis_index("xh") * 2 + lax.axis_index("xl"), lax.axis_index("y")


def row_of(sibling, couple, unit):
    core, my_x, my_y = here()
    side = 1 - core if sibling else core
    my_half = lax.div(my_x, 2)
    along_y = unit * 2 + (my_half ^ couple)
    along_x = (my_y ^ (2 * couple + unit // 2)) * 2 + unit % 2
    return side * GROUPS + jnp.where(side == 0, along_y, along_x)


def score_kernel(sibling, couple, cents, blocks, *refs):
    points_t, scores, stat = refs[-3:]
    core, my_x, my_y = here()
    side = 1 - core if sibling else core
    for at, (second, which) in enumerate(BLOCKS[couple]):
        x, y = lax.rem(my_x + second, 4), lax.rem(my_y + second, 4)
        unit = jnp.where(side == 0, y, which * 2 + lax.div(x, 2))
        low = jnp.where(side == 0, lax.rem(my_x, 2) ^ which, lax.rem(x, 2))
        points_t[unit, :, low] = blocks[at]
    part = cents.shape[0] // CHUNKS
    logs = []
    for pair in range(UNITS // 2):
        block = rows_of(points_t, pair)
        tops, totals = [], []
        for chunk in range(CHUNKS):
            rows = pl.ds(chunk * part, part)
            value = jnp.dot(cents[rows, :], block, preferred_element_type=jnp.float32) * SHARP2
            top = jnp.max(value, axis=0, keepdims=True)
            scores[pair, rows, :] = value
            tops.append(top)
            totals.append(jnp.sum(jnp.exp2(value - top), axis=0, keepdims=True))
        top = functools.reduce(jnp.maximum, tops)
        total = sum(s * jnp.exp2(t - top) for t, s in zip(tops, totals))
        log = top + jnp.log2(total)
        logs += [log[:, :HALF], log[:, HALF:]]
    if (sibling, couple) != COUPLES[-1]:
        stat[...] = jnp.concatenate(logs, axis=0)
        return
    parts = [[ref[pl.ds(u, 1), :] for u in range(UNITS)] for ref in refs[:-3]] + [logs]
    for (other, second_couple), values in zip(COUPLES, parts):
        for unit, value in enumerate(values):
            stat[pl.ds(row_of(other, second_couple, unit), 1), :] = value


def merged(stats):
    values = [stats[i] for i in range(stats.shape[0])]
    top = functools.reduce(jnp.maximum, values)
    return top + jnp.log2(functools.reduce(jnp.add, [jnp.exp2(v - top) for v in values]))


def chip_kernel(mine, other, stat):
    core = lax.axis_index("core")
    a = jnp.where(core == 0, mine[...], other[...])
    b = jnp.where(core == 0, other[...], mine[...])
    top = jnp.maximum(a, b)
    stat[...] = top + jnp.log2(jnp.exp2(a - top) + jnp.exp2(b - top))


def merge_kernel(stats, *refs):
    refs[len(refs) // 2][...] = merged(stats)


def pull_kernel(stats, cents, *refs):
    big, (out, own_rows, log_part, block, sems) = refs[:-5], refs[-5:]
    core, my_x, my_y = here()
    log_part[...] = merged(stats)
    group = my_y * 2 + lax.div(my_x, 2)
    for side in range(2):
        half = log_part[pl.ds(side * GROUPS + group, 1), :]
        own_rows[:, side * HALF : (side + 1) * HALF] = half * LN2
    work = []
    for index, (sibling, couple) in enumerate(COUPLES):
        for pair in range(UNITS // 2):
            logs = [log_part[pl.ds(row_of(sibling, couple, 2 * pair + i), 1), :] for i in range(2)]
            work.append((big[2 * index], big[2 * index + 1], pair, jnp.concatenate(logs, axis=1)))
    part = cents.shape[0] // CHUNKS
    copies = []
    for chunk in range(CHUNKS):
        rows = pl.ds(chunk * part, part)
        acc, mass = 0.0, 0.0
        for points_t, scores, pair, log_rows in work:
            weights = jnp.exp2(scores[pair, rows, :] - log_rows).astype(jnp.bfloat16)
            acc = acc + lax.dot_general(
                weights,
                rows_of(points_t, pair),
                (((1,), (1,)), ((), ())),
                preferred_element_type=jnp.float32,
            )
            mass = mass + jnp.sum(weights.astype(jnp.float32), axis=1, keepdims=True)
        value = (cents[rows, :].astype(jnp.float32) + acc) / (1.0 + mass)
        block[rows, :] = value.astype(jnp.bfloat16)
        copies.append(pltpu.make_async_copy(block.at[rows], out.at[rows], sems.at[chunk]))
        copies[-1].start()
    for copy in copies:
        copy.wait()


def gather(points):
    feats = points.T
    halves = jnp.stack([feats[:, :HALF], feats[:, HALF:]])
    sent = jnp.broadcast_to(halves[None], (8,) + halves.shape).reshape((16,) + halves.shape[1:])
    block = lax.all_to_all(sent, ("z", "core"), 0, 0, tiled=True).reshape(8, 48, HALF)
    one, two, three = [receive(block, crossed(FIRST, k)) for k in (1, 2, 3)]
    couples = []
    for couple, steps in zip(([block, one], [two, three]), STEPS):
        couple = jnp.stack(couple)
        pieces = [couple] + [receive(couple, shifted(SECOND, k)) for k in steps]
        couples.append(pieces)
    return [jnp.concatenate(pieces) for pieces in lax.optimization_barrier(couples)]


def spread(value, axes, count):
    copies = jnp.broadcast_to(value[None], (count,) + value.shape)
    return lax.all_to_all(copies, axes, 0, 0, tiled=True)


def kept_in_vmem(value):
    return pltpu.with_memory_space_constraint(value, pltpu.VMEM)


def limit(megabytes):
    return pltpu.CompilerParams(vmem_limit_bytes=megabytes * 1024 * 1024)


def per_device(points, centroids):
    kept = centroids.shape[0]
    vmem = pl.BlockSpec(memory_space=pltpu.VMEM)
    points_shape = pltpu.VMEM((UNITS, 8, 2, 48, HALF), jnp.bfloat16)
    scores_shape = pltpu.VMEM((UNITS // 2, kept, ROWS), jnp.float32)
    stat_shape = jax.ShapeDtypeStruct((2 * GROUPS, HALF), jnp.float32)
    unit_shape = jax.ShapeDtypeStruct((UNITS, HALF), jnp.float32)

    big, stats = [], []
    own = gather(points)
    for sibling, couple in COUPLES:
        blocks = receive(own[couple], SWAP) if sibling else own[couple]
        last = (sibling, couple) == COUPLES[-1]
        earlier = stats if last else []
        points_t, scores, stat = pl.pallas_call(
            functools.partial(score_kernel, sibling, couple),
            out_shape=(points_shape, scores_shape, stat_shape if last else unit_shape),
            in_specs=[vmem] * (2 + len(earlier)),
            out_specs=(vmem,) * 3,
            compiler_params=limit(12),
            name=("sibling" if sibling else "own") + str(couple),
        )(centroids, kept_in_vmem(blocks), *earlier)
        big += [points_t, scores]
        stats.append(stat)

    mine = stats[-1]
    stat = pl.pallas_call(
        chip_kernel,
        out_shape=stat_shape,
        in_specs=[vmem] * 2,
        out_specs=vmem,
        compiler_params=limit(2),
        name="chip",
    )(mine, receive(mine, SWAP))

    shapes = [points_shape, scores_shape] * len(COUPLES)
    stat, *big = pl.pallas_call(
        merge_kernel,
        out_shape=(stat_shape, *shapes),
        in_specs=[vmem] * (1 + len(big)),
        out_specs=(vmem,) * (1 + len(big)),
        input_output_aliases={i: i for i in range(1, 1 + len(big))},
        compiler_params=limit(24),
        name="merge",
    )(spread(stat, ("z",), 8), *[kept_in_vmem(v) for v in big])

    updated, own_rows = pl.pallas_call(
        pull_kernel,
        out_shape=(
            jax.ShapeDtypeStruct((kept, D), jnp.bfloat16),
            jax.ShapeDtypeStruct((1, ROWS), jnp.float32),
        ),
        in_specs=[vmem] * (2 + len(big)),
        out_specs=(pl.BlockSpec(memory_space=pl.ANY), vmem),
        scratch_shapes=[
            pltpu.VMEM((2 * GROUPS, HALF), jnp.float32),
            pltpu.VMEM((kept, D), jnp.bfloat16),
            pltpu.SemaphoreType.DMA((CHUNKS,)),
        ],
        compiler_params=limit(24),
        name="pull",
    )(spread(stat, ("xl", "y", "xh"), 16), centroids, *[kept_in_vmem(v) for v in big])
    return updated, own_rows.reshape(ROWS)


def solution(mesh):
    fine = Mesh(mesh.devices.reshape([SIZES[a] for a in AXES]), AXES)
    return jax.shard_map(
        per_device,
        mesh=fine,
        in_specs=(P(("y", "xh"), ("z", "xl", "core")), P(AXES, None)),
        out_specs=(P(AXES, None), P(("y", "xh"))),
        check_vma=False,
    )
```
